32 devices in a mesh: subj: 4 (over x, core), obj: 8 (over z, y).
Axes of the slice: x: 2, y: 2, z: 4, core: 2. Of those that a mesh axis runs over, the one named last changes fastest.
Arguments:
- subject_factors: bfloat16 [2048, 512], P(('subj', 'obj')), may hold values from -6 to 6
- object_factors: bfloat16 [4096, 512], P(('obj', 'subj')), may hold values from -6 to 6
- relations: bfloat16 [2, 512, 512], P(None, 'subj', 'obj'), may hold values from -0.01171875 to 0.01171875
- labels: int32 [2, 2048, 4096], P(None, 'subj', 'obj'), may hold values from 0 to 2
Outputs:
- grad_subject: float32 [2048, 512], P(('subj', 'obj'))
- grad_object: float32 [4096, 512], P(('obj', 'subj'))
- grad_relations: float32 [2, 512, 512], P(None, 'subj', 'obj')
- loss_rows: float32 [2048], P(('subj', 'obj'))
The draws below stay inside these ranges and needn't reach their ends.
All inputs are finite; a program needn't handle non-finite values.
Results may differ from the reference program's by a relative error of at most 0.02.
Values may be sent and summed in bfloat16 or wider, within the bound.
A program may use at most 64 MiB of HBM per device.

```python
import jax
import jax.numpy as jnp
from jax import lax

RANK = 512
RELS = 2
SUB_DEV = 512
OBJ_DEV = 512
SUBJECTS = 2048
OBJECTS = 4096
N_SUBJ = 4
N_OBJ = 8


def with_ends(entries, key, least, largest):
    extent = entries.shape
    spot = [jax.random.randint(jax.random.fold_in(key, axis), (), 0, extent[axis]) for axis in range(len(extent))]
    entries = entries.at[tuple(spot)].set(least)
    longest = extent.index(max(extent))
    spot[longest] = (spot[longest] + 1) % extent[longest]
    return entries.at[tuple(spot)].set(largest)


def steps_of(rng, shape, split, smallest, top_value):
    loudness = 1.0
    for dim, shards_of in split:
        draws = jax.random.uniform(jax.random.fold_in(jax.random.fold_in(rng, 6), dim), (shards_of,), jnp.float32, smallest / len(split), top_value / len(split))
        loudness = loudness * jnp.repeat(jnp.exp(draws), shape[dim] // shards_of).reshape((-1,) + (1,) * (len(shape) - 1 - dim))
    return loudness


def bell_draw(rng, shape, deviation, reach, cuts=(), held_as=jnp.bfloat16):
    array = jax.random.normal(rng, shape, jnp.float32) * deviation
    if len(cuts) > 0:
        array = steps_of(rng, shape, cuts, -0.22, 0.18) * array
    return jnp.clip(array, min=-reach, max=reach).astype(held_as)


def setup_inputs(seed: int = 0) -> dict:
    keys = jax.random.split(jax.random.key(seed), 5)
    subject_factors = bell_draw(keys[0], (SUBJECTS, RANK), 1.0, 6.0, ((0, 32),))
    object_factors = bell_draw(keys[1], (OBJECTS, RANK), 1.0, 6.0, ((0, 32),))
    relations = bell_draw(keys[2], (RELS, RANK, RANK), (RANK * RANK) ** -0.5, 0.01171875, ((1, 4), (2, 8)))
    labels = with_ends(jax.random.randint(keys[3], (RELS, SUBJECTS, OBJECTS), 0, 3), jax.random.fold_in(keys[3], 1), 0, 2).astype(jnp.int32)
    return dict(subject_factors=subject_factors, object_factors=object_factors, relations=relations, labels=labels)


def reference(subject_factors, object_factors, relations, labels):
    subject_f = subject_factors.astype(jnp.float32)
    object_f = object_factors.astype(jnp.float32)
    relation_f = relations.astype(jnp.float32)
    left = jnp.einsum("ic,kca->kia", subject_f, relation_f).astype(jnp.bfloat16).astype(jnp.float32)
    right = jnp.einsum("jc,kac->kja", object_f, relation_f).astype(jnp.bfloat16).astype(jnp.float32)
    left_blocks = left.reshape(RELS, N_SUBJ, SUB_DEV, RANK)

    def per_block(carry, block):
        subject_acc, loss_acc, relation_acc = carry
        start = (block * OBJ_DEV).astype(jnp.int32)
        object_part = lax.dynamic_slice_in_dim(object_f, start, OBJ_DEV, 0)
        right_part = lax.dynamic_slice_in_dim(right, start, OBJ_DEV, 1)
        label_part = lax.dynamic_slice_in_dim(labels, start, OBJ_DEV, 2)
        scores = jnp.einsum("kia,ja->kij", left, object_part)
        target = (label_part == 2).astype(jnp.float32)
        weight = (label_part > 0).astype(jnp.float32)
        cell_loss = weight * (jax.nn.softplus(scores) - target * scores)
        residual = (weight * (jax.nn.sigmoid(scores) - target)).astype(jnp.bfloat16).astype(jnp.float32)
        loss_part = (jnp.sum(cell_loss, axis=(0, 2)) / (RELS * OBJECTS)).astype(jnp.bfloat16).astype(jnp.float32)
        subject_part = jnp.einsum("kij,kja->ia", residual, right_part).astype(jnp.bfloat16).astype(jnp.float32)
        residual_blocks = residual.reshape(RELS, N_SUBJ, SUB_DEV, OBJ_DEV)
        object_terms = jnp.einsum("knsj,knsa->nja", residual_blocks, left_blocks)
        object_grad = jnp.sum(object_terms.astype(jnp.bfloat16).astype(jnp.float32), axis=0)
        carried = jnp.einsum("kij,ja->kia", residual, object_part).astype(jnp.bfloat16).astype(jnp.float32)
        relation_part = jnp.einsum("ic,kia->kca", subject_f, carried)
        return (subject_acc + subject_part, loss_acc + loss_part, relation_acc + relation_part), object_grad

    start_carry = (jnp.zeros((SUBJECTS, RANK), jnp.float32), jnp.zeros((SUBJECTS,), jnp.float32),
                   jnp.zeros((RELS, RANK, RANK), jnp.float32))
    final, object_grads = lax.scan(per_block, start_carry, jnp.arange(N_OBJ, dtype=jnp.int32))
    subject_grad, loss_rows, relation_grad = final
    grad_object = object_grads.reshape(OBJECTS, RANK)
    return subject_grad, grad_object, relation_grad / SUBJECTS, loss_rows
```

```python
import functools

import jax
import jax.numpy as jnp
from jax import lax
from jax.experimental import pallas as pl
from jax.experimental.pallas import tpu as pltpu
from jax.sharding import PartitionSpec as P

F32 = jnp.float32
BF16 = jnp.bfloat16
PAIR = 2
LANES = 128
CHUNK = 128


def mm(a, b, ca, cb):
    return lax.dot_general(a, b, (((ca,), (cb,)), ((), ())), preferred_element_type=F32)


def kernel(
    nx, nh, copies,
    s_hbm, o_hbm, r_in, lab_hbm,
    gs_out, go_out, gr_out, loss_out,
    s_all, o_all, r_own, r_all, r_full, labels, left, right, resid, carried,
    gsub, gr, gr_crx, gr_tx, gr_xrx, gr_ytx, gr_yrx, gr_ztx, gr_zrx,
    go, go_crx, go_tx, go_xrx, gs, gs_yrx, gs_ztx, gs_zrx,
    send_sem, recv_sem, local_sem,
):
    subj = lax.axis_index("subj")
    obj = lax.axis_index("obj")
    x, c = subj // PAIR, subj % PAIR
    z, y = obj // PAIR, obj % PAIR
    oc, oy = 1 - c, 1 - y
    rels, rank = r_full.shape[0], r_full.shape[1]
    rows_r, wid = r_in.shape[1], r_in.shape[2]
    rows_s = s_all.shape[2]
    ns = nh * PAIR * rows_s
    no = nx * PAIR * o_all.shape[2]
    core_dev = (x * PAIR + oc, obj)
    y_dev = (subj, z * PAIR + oy)

    def xs(e):
        return lax.rem(x + e, nx)

    def zs(d):
        return lax.rem(z + d, nh)

    def x_from(e):
        return lax.rem(x - e + nx, nx)

    def z_from(d):
        return lax.rem(z - d + nh, nh)

    def x_dev(e):
        return (xs(e) * PAIR + c, obj)

    def z_dev(d):
        return (subj, zs(d) * PAIR + y)

    started = []

    def send(src, dst, dev):
        i = len(started)
        cp = pltpu.make_async_remote_copy(
            src_ref=src, dst_ref=dst, send_sem=send_sem.at[i], recv_sem=recv_sem.at[i],
            device_id=dev, device_id_type=pl.DeviceIdType.MESH,
        )
        cp.start()
        started.append(cp)
        return cp

    lab_cp = pltpu.make_async_copy(lab_hbm, labels, local_sem.at[0])
    lab_cp.start()
    s_cp = pltpu.make_async_copy(s_hbm, s_all.at[z, y], local_sem.at[1])
    s_cp.start()
    o_cp = pltpu.make_async_copy(o_hbm, o_all.at[x, c], local_sem.at[2])
    o_cp.start()
    for k in range(rels):
        r_own[:, k * wid:(k + 1) * wid] = r_in[k]
    r_cp = pltpu.make_async_copy(r_own, r_all.at[z, y, x, c], local_sem.at[3])
    r_cp.start()

    barrier = pltpu.get_barrier_semaphore()
    partners = [core_dev, y_dev] + [x_dev(e) for e in range(1, nx)] + [z_dev(d) for d in range(1, nh)]
    for dev in partners:
        pl.semaphore_signal(barrier, inc=1, device_id=dev, device_id_type=pl.DeviceIdType.MESH)
    pl.semaphore_wait(barrier, len(partners))

    order = [d for d in range(nh)]
    rz, sz = {}, {}
    for d in range(1, nh):
        rz[d] = send(r_own, r_all.at[z, y, x, c], z_dev(d))
    for d in range(1, nh):
        sz[d] = send(s_hbm, s_all.at[z, y], z_dev(d))
    ox = {e: send(o_hbm, o_all.at[x, c], x_dev(e)) for e in range(1, nx)}
    ocr = {0: send(o_hbm, o_all.at[x, c], core_dev)}
    ry, sy = {}, {}
    ry[0] = send(r_own, r_all.at[z, y, x, c], y_dev)
    sy[0] = send(s_hbm, s_all.at[z, y], y_dev)
    r_cp.wait()
    rx, rc = {}, {}

    def spread(d):
        blk = r_all.at[z_from(d), :, x, c]
        for e in range(1, nx):
            rx[d, e] = send(blk, blk, x_dev(e))
        rc[d, 0] = send(blk, blk, core_dev)

    for d in order[1:]:
        rz[d].wait_recv()
        blk = r_all.at[z_from(d), y, x, c]
        ry[d] = send(blk, blk, y_dev)
    for d in order:
        ry[d].wait_recv()
        spread(d)
    for e in range(1, nx):
        ox[e].wait_recv()
        blk = o_all.at[x_from(e), c]
        ocr[e] = send(blk, blk, core_dev)
    for d in order[1:]:
        sz[d].wait_recv()
        blk = s_all.at[z_from(d), y]
        sy[d] = send(blk, blk, y_dev)
    for d in order:
        for e in range(1, nx):
            rx[d, e].wait_recv()
            blk = r_all.at[z_from(d), :, x_from(e), c]
            rc[d, e] = send(blk, blk, core_dev)
    for key in rc:
        rc[key].wait_recv()
    for o in range(nh * PAIR):
        v = r_all[o // PAIR, o % PAIR].reshape(rank, rels * wid)
        for k in range(rels):
            r_full[k, :, o * wid:(o + 1) * wid] = v[:, k * wid:(k + 1) * wid]
    s_cp.wait()
    for d in order:
        sy[d].wait_recv()
    s_blk = s_all[...].reshape(ns, rank)
    for k in range(rels):
        left[k] = mm(s_blk, r_full[k], 1, 0).astype(BF16)
    o_cp.wait()
    for e in range(nx):
        ocr[e].wait_recv()
    lab_cp.wait()

    gsub[:, rank:] = jnp.zeros((ns, LANES), F32)
    for k in range(rels):
        def rows_body(i, carry, k=k):
            r = pl.ds(pl.multiple_of(i * CHUNK, CHUNK), CHUNK)
            ob = o_all[...].reshape(no, rank)
            sc = mm(left[k, r, :], ob, 1, 1)
            codes = labels[k, r, :]
            edge = codes == 2
            target = jnp.where(edge, 1.0, 0.0).astype(F32)
            weight = jnp.where(codes > 0, 1.0, 0.0).astype(F32)
            e = jnp.exp(-jnp.abs(sc))
            inv = 1.0 / (1.0 + e)
            sig = jnp.where(sc >= 0, inv, e * inv)
            soft = jnp.maximum(sc, 0.0) + jnp.log1p(e)
            cell = weight * (soft - target * sc)
            gsub[r, rank:] += jnp.broadcast_to(
                jnp.sum(cell, axis=1, keepdims=True), (CHUNK, LANES))
            res = (weight * (sig - target)).astype(BF16)
            resid[k, r, :] = res
            carried[k, r, :] = mm(res, ob, 1, 0).astype(BF16)
            return carry
        lax.fori_loop(0, ns // CHUNK, rows_body, 0)
        term = mm(s_all[...].reshape(ns, rank), carried[k], 0, 0).astype(BF16)
        for o in range(nh * PAIR):
            gr[o % PAIR, o // PAIR, :, :, :, k * wid:(k + 1) * wid] = (
                term[:, o * wid:(o + 1) * wid].reshape(nx, PAIR, rows_r, wid))

    grc = {}
    for e in list(range(1, nx)) + [0]:
        grc[e] = send(gr.at[:, :, xs(e), oc], gr_crx.at[e], core_dev)

    acc = mm(resid[0], left[0], 0, 0)
    for k in range(1, rels):
        acc = acc + mm(resid[k], left[k], 0, 0)
    go[...] = acc.astype(BF16).reshape(go.shape)
    goc = {}
    for e in list(range(1, nx)) + [0]:
        goc[e] = send(go.at[xs(e), oc], go_crx.at[e], core_dev)

    grx = {}
    for e in range(1, nx):
        grc[e].wait_recv()
        for first in (1, 0):
            q = oy if first else y
            gr_tx[e, q] = (gr[q, :, xs(e), c].astype(F32) + gr_crx[e, q].astype(F32)).astype(BF16)
            grx[e, first] = send(gr_tx.at[e, q], gr_xrx.at[e, q], x_dev(e))

    ob = o_all[...].reshape(no, rank)
    for k in range(rels):
        right[k] = mm(ob, r_full[k], 1, 1).astype(BF16)
    acc = mm(resid[0], right[0], 1, 0)
    for k in range(1, rels):
        acc = acc + mm(resid[k], right[k], 1, 0)
    objects = no * nh * PAIR
    gs[:, :, :, :rank] = acc.astype(BF16).reshape(nh, PAIR, rows_s, rank)
    gs[:, :, :, rank:] = (gsub[:, rank:] / (rels * objects)).astype(BF16).reshape(nh, PAIR, rows_s, LANES)
    gsy = {}
    for d in order[1:] + [0]:
        gsy[d] = send(gs.at[zs(d), oy], gs_yrx.at[d], y_dev)

    gox = {}
    for e in range(1, nx):
        goc[e].wait_recv()
        go_tx[e] = (go[xs(e), c].astype(F32) + go_crx[e].astype(F32)).astype(BF16)
        gox[e] = send(go_tx.at[e], go_xrx.at[e], x_dev(e))

    grc[0].wait_recv()
    for e in range(1, nx):
        grx[e, 1].wait_recv()
    t = gr[oy, :, x, c].astype(F32) + gr_crx[0, oy].astype(F32)
    for e in range(1, nx):
        t = t + gr_xrx[e, oy].astype(F32)
    gr_ytx[...] = t.astype(BF16)
    gry = send(gr_ytx, gr_yrx, y_dev)

    gsz = {}
    for d in order[1:]:
        gsy[d].wait_recv()
        gs_ztx[d] = (gs[zs(d), y].astype(F32) + gs_yrx[d].astype(F32)).astype(BF16)
        gsz[d] = send(gs_ztx.at[d], gs_zrx.at[d], z_dev(d))

    for e in range(1, nx):
        grx[e, 0].wait_recv()
    gry.wait_recv()

    def gr_sum(zz):
        t = gr[y, zz, x, c].astype(F32) + gr_crx[0, y, zz].astype(F32)
        for e in range(1, nx):
            t = t + gr_xrx[e, y, zz].astype(F32)
        return t + gr_yrx[zz].astype(F32)

    grz = {}
    for d in order[1:]:
        gr_ztx[d] = gr_sum(zs(d)).astype(BF16)
        grz[d] = send(gr_ztx.at[d], gr_zrx.at[d], z_dev(d))

    goc[0].wait_recv()
    t = go[x, c].astype(F32) + go_crx[0].astype(F32)
    for e in range(1, nx):
        gox[e].wait_recv()
        t = t + go_xrx[e].astype(F32)
    go_out[...] = t
    gsy[0].wait_recv()
    t = gs[z, y].astype(F32) + gs_yrx[0].astype(F32)
    for d in order[1:]:
        gsz[d].wait_recv()
        t = t + gs_zrx[d].astype(F32)
    gs_out[...] = t[:, :rank]
    loss_out[...] = t[:, rank:]
    t = gr_sum(z)
    for d in order[1:]:
        grz[d].wait_recv()
        t = t + gr_zrx[d].astype(F32)
    t = t / (ns * nx * PAIR)
    for k in range(rels):
        gr_out[k] = t[:, k * wid:(k + 1) * wid]
    for cp in started:
        cp.wait_send()


def body(subject_factors, object_factors, relations, labels):
    n_subj, n_obj = lax.axis_size("subj"), lax.axis_size("obj")
    nx, nh = n_subj // PAIR, n_obj // PAIR
    rows_s, rank = subject_factors.shape
    rows_o = object_factors.shape[0]
    rels, rows_r, wid = relations.shape
    pack = rels * wid
    ns, no = rows_s * n_obj, rows_o * n_subj
    copies = 64 + 4 * nh + 8 * nx + 3 * nh * nx
    v = pltpu.VMEM
    scratch = [
        v((nh, PAIR, rows_s, rank), BF16),
        v((nx, PAIR, rows_o, rank), BF16),
        v((rows_r, pack), BF16),
        v((nh, PAIR, nx, PAIR, rows_r, pack), BF16),
        v((rels, rank, rank), BF16),
        v(labels.shape, jnp.int32),
        v((rels, ns, rank), BF16),
        v((rels, no, rank), BF16),
        v((rels, ns, no), BF16),
        v((rels, ns, rank), BF16),
        v((ns, rank + LANES), F32),
        v((PAIR, nh, nx, PAIR, rows_r, pack), BF16),
        v((nx, PAIR, nh, rows_r, pack), BF16),
        v((nx, PAIR, nh, rows_r, pack), BF16),
        v((nx, PAIR, nh, rows_r, pack), BF16),
        v((nh, rows_r, pack), BF16),
        v((nh, rows_r, pack), BF16),
        v((nh, rows_r, pack), BF16),
        v((nh, rows_r, pack), BF16),
        v((nx, PAIR, rows_o, rank), BF16),
        v((nx, rows_o, rank), BF16),
        v((nx, rows_o, rank), BF16),
        v((nx, rows_o, rank), BF16),
        v((nh, PAIR, rows_s, rank + LANES), BF16),
        v((nh, rows_s, rank + LANES), BF16),
        v((nh, rows_s, rank + LANES), BF16),
        v((nh, rows_s, rank + LANES), BF16),
        pltpu.SemaphoreType.DMA((copies,)),
        pltpu.SemaphoreType.DMA((copies,)),
        pltpu.SemaphoreType.DMA((4,)),
    ]
    hbm = pl.BlockSpec(memory_space=pl.ANY)
    vm = pl.BlockSpec(memory_space=pltpu.VMEM)
    grad_subject, grad_object, grad_relations, loss = pl.pallas_call(
        functools.partial(kernel, nx, nh, copies),
        out_shape=(
            jax.ShapeDtypeStruct((rows_s, rank), F32),
            jax.ShapeDtypeStruct((rows_o, rank), F32),
            jax.ShapeDtypeStruct((rels, rows_r, wid), F32),
            jax.ShapeDtypeStruct((rows_s, LANES), F32),
        ),
        in_specs=[hbm, hbm, vm, hbm],
        out_specs=(vm, vm, vm, vm),
        scratch_shapes=scratch,
        compiler_params=pltpu.CompilerParams(
            collective_id=0, has_side_effects=True, vmem_limit_bytes=48 * 1024 * 1024
        ),
    )(subject_factors, object_factors, relations, labels)
    return grad_subject, grad_object, grad_relations, loss[:, 0]


def solution(mesh):
    placed = (
        P(("subj", "obj"), None),
        P(("obj", "subj"), None),
        P(None, "subj", "obj"),
        P(None, "subj", "obj"),
    )
    return jax.shard_map(
        body,
        mesh=mesh,
        in_specs=placed,
        out_specs=(
            P(("subj", "obj"), None),
            P(("obj", "subj"), None),
            P(None, "subj", "obj"),
            P(("subj", "obj")),
        ),
        check_vma=False,
    )
```

```python
import functools

import jax
import jax.numpy as jnp
from jax import lax
from jax.experimental import pallas as pl
from jax.experimental.pallas import tpu as pltpu
from jax.sharding import PartitionSpec as P

F32 = jnp.float32
BF16 = jnp.bfloat16
PAIR = 2
LANES = 128
CHUNK = 64


def mm(a, b, ca, cb):
    return lax.dot_general(a, b, (((ca,), (cb,)), ((), ())), preferred_element_type=F32)


def kernel(
    nx, nh,
    s_hbm, o_hbm, r_hbm, lab_hbm,
    gs_out, go_out, gr_out,
    s_all, o_all, r_all, r_full, labels, left, right, score, resid, carried,
    loss, gr, gr_crx, gr_tx, gr_xrx, gr_ytx, gr_yrx, gr_ztx, gr_zrx,
    go, go_crx, go_tx, go_xrx, gs, gs_yrx, gs_ztx, gs_zrx,
    send_sem, recv_sem, local_sem,
):
    subj = lax.axis_index("subj")
    obj = lax.axis_index("obj")
    x, c = subj // PAIR, subj % PAIR
    z, y = obj // PAIR, obj % PAIR
    oc, oy = 1 - c, 1 - y
    rels, rank = r_full.shape[0], r_full.shape[1]
    wid, rows_r = r_hbm.shape[1], r_hbm.shape[2]
    rows_s = s_all.shape[2]
    ns = nh * PAIR * rows_s
    no = nx * PAIR * o_all.shape[2]
    core_dev = (x * PAIR + oc, obj)
    y_dev = (subj, z * PAIR + oy)

    def xs(e):
        return lax.rem(x + e, nx)

    def zs(d):
        return lax.rem(z + d, nh)

    def x_from(e):
        return lax.rem(x - e + nx, nx)

    def z_from(d):
        return lax.rem(z - d + nh, nh)

    def x_dev(e):
        return (xs(e) * PAIR + c, obj)

    def z_dev(d):
        return (subj, zs(d) * PAIR + y)

    started = []

    def send(src, dst, dev):
        i = len(started)
        cp = pltpu.make_async_remote_copy(
            src_ref=src, dst_ref=dst, send_sem=send_sem.at[i], recv_sem=recv_sem.at[i],
            device_id=dev, device_id_type=pl.DeviceIdType.MESH,
        )
        cp.start()
        started.append(cp)
        return cp

    barrier = pltpu.get_barrier_semaphore()
    partners = [core_dev, y_dev] + [x_dev(e) for e in range(1, nx)] + [z_dev(d) for d in range(1, nh)]
    for dev in partners:
        pl.semaphore_signal(barrier, inc=1, device_id=dev, device_id_type=pl.DeviceIdType.MESH)

    r_cp = pltpu.make_async_copy(r_hbm, r_all.at[z, y, x, c], local_sem.at[3])
    r_cp.start()
    s_cp = pltpu.make_async_copy(s_hbm, s_all.at[z, y], local_sem.at[1])
    s_cp.start()
    o_cp = pltpu.make_async_copy(o_hbm, o_all.at[x, c], local_sem.at[2])
    o_cp.start()
    lab_cp = pltpu.make_async_copy(lab_hbm, labels, local_sem.at[0])
    lab_cp.start()
    loss[...] = jnp.zeros_like(loss)
    pl.semaphore_wait(barrier, len(partners))

    order = [d for d in range(nh)]
    rz, sz = {}, {}
    for d in range(1, nh):
        rz[d] = send(r_hbm, r_all.at[z, y, x, c], z_dev(d))
    ry, sy = {}, {}
    ry[0] = send(r_hbm, r_all.at[z, y, x, c], y_dev)
    ox = {e: send(o_hbm, o_all.at[x, c], x_dev(e)) for e in range(1, nx)}
    ocr = {0: send(o_hbm, o_all.at[x, c], core_dev)}
    for d in range(1, nh):
        sz[d] = send(s_hbm, s_all.at[z, y], z_dev(d))
    sy[0] = send(s_hbm, s_all.at[z, y], y_dev)
    r_cp.wait()
    rx, rc = {}, {}

    def spread(d):
        ry[d].wait_recv()
        blk = r_all.at[z_from(d), :, x, c]
        for e in range(1, nx):
            rx[d, e] = send(blk, blk, x_dev(e))
        rc[d, 0] = send(blk, blk, core_dev)

    for d in order:
        if d:
            rz[d].wait_recv()
            blk = r_all.at[z_from(d), y, x, c]
            ry[d] = send(blk, blk, y_dev)
        if d != 1:
            spread(d - 1 if d else 0)
    if nh > 1:
        spread(nh - 1)
    for e in range(1, nx):
        ox[e].wait_recv()
        blk = o_all.at[x_from(e), c]
        ocr[e] = send(blk, blk, core_dev)
    for d in order[1:]:
        sz[d].wait_recv()
        blk = s_all.at[z_from(d), y]
        sy[d] = send(blk, blk, y_dev)
    for d in order:
        for e in range(1, nx):
            rx[d, e].wait_recv()
            blk = r_all.at[z_from(d), :, x_from(e), c]
            rc[d, e] = send(blk, blk, core_dev)
    for key in rc:
        rc[key].wait_recv()
    for s in range(nx * PAIR):
        for k in range(rels):
            r_full[k, :, s * rows_r:(s + 1) * rows_r] = (
                r_all[:, :, s // PAIR, s % PAIR, k].reshape(rank, rows_r))
    s_cp.wait()
    for d in order:
        sy[d].wait_recv()
    for k in range(rels):
        left[k] = mm(s_all[...].reshape(ns, rank), r_full[k], 1, 1).astype(BF16)
    o_cp.wait()
    for e in range(nx):
        ocr[e].wait_recv()
    score[...] = mm(
        left[...].reshape(rels * ns, rank), o_all[...].reshape(no, rank), 1, 1
    ).reshape(rels, ns, no)
    lab_cp.wait()

    for k in range(rels):
        def rows_body(i, carry, k=k):
            r = pl.ds(pl.multiple_of(i * CHUNK, CHUNK), CHUNK)
            sc = score[k, r, :]
            codes = labels[k, r, :]
            target = jnp.where(codes == 2, 1.0, 0.0).astype(F32)
            held = codes > 0
            e = jnp.exp(-jnp.abs(sc))
            inv = 1.0 / (1.0 + e)
            sig = jnp.where(sc >= 0, inv, e * inv)
            soft = jnp.maximum(sc, 0.0) + jnp.log1p(e)
            cell = jnp.where(held, soft - target * sc, 0.0)
            part = loss[r, :]
            for g in range(no // LANES):
                part = part + cell[:, g * LANES:(g + 1) * LANES]
            loss[r, :] = part
            resid[k, r, :] = jnp.where(held, sig - target, 0.0).astype(BF16)
            return carry
        lax.fori_loop(0, ns // CHUNK, rows_body, 0)

    carried[...] = mm(
        resid[...].reshape(rels * ns, no), o_all[...].reshape(no, rank), 1, 0
    ).astype(BF16).reshape(rels, ns, rank)
    for k in range(rels):
        term = mm(carried[k], s_all[...].reshape(ns, rank), 0, 0).astype(BF16)
        for s in range(nx * PAIR):
            gr[:, :, s // PAIR, s % PAIR, k] = (
                term[:, s * rows_r:(s + 1) * rows_r].reshape(nh, PAIR, wid, rows_r))
    grc = {}
    for e in list(range(1, nx)) + [0]:
        grc[e] = send(gr.at[:, :, xs(e), oc], gr_crx.at[e], core_dev)

    acc = None
    for k in range(rels):
        right[k] = mm(o_all[...].reshape(no, rank), r_full[k], 1, 0).astype(BF16)
        t = mm(resid[k], right[k], 1, 0)
        acc = t if acc is None else acc + t
    objects = no * nh * PAIR
    gs[:, :, :, :rank] = acc.astype(BF16).reshape(nh, PAIR, rows_s, rank)
    row_loss = jnp.sum(loss[...], axis=1, keepdims=True) / (rels * objects)
    gs[:, :, :, rank:] = jnp.broadcast_to(row_loss, (ns, LANES)).astype(BF16).reshape(
        nh, PAIR, rows_s, LANES)
    gsy = {}
    for d in order[1:] + [0]:
        gsy[d] = send(gs.at[zs(d), oy], gs_yrx.at[d], y_dev)

    grx = {}
    for e in range(1, nx):
        grc[e].wait_recv()
        for first in (1, 0):
            q = oy if first else y
            gr_tx[e, q] = (gr[:, q, xs(e), c].astype(F32) + gr_crx[e, :, q].astype(F32)).astype(BF16)
            grx[e, first] = send(gr_tx.at[e, q], gr_xrx.at[e, q], x_dev(e))

    acc = None
    for k in range(rels):
        t = mm(resid[k], left[k], 0, 0)
        acc = t if acc is None else acc + t
    go[...] = acc.astype(BF16).reshape(go.shape)
    goc = {}
    for e in list(range(1, nx)) + [0]:
        goc[e] = send(go.at[xs(e), oc], go_crx.at[e], core_dev)

    def gr_sum(d, q):
        t = gr[zs(d), q, x, c].astype(F32) + gr_crx[0, zs(d), q].astype(F32)
        for e in range(1, nx):
            t = t + gr_xrx[e, q, zs(d)].astype(F32)
        return t

    gox = {}
    for e in range(1, nx):
        goc[e].wait_recv()
        go_tx[e] = (go[xs(e), c].astype(F32) + go_crx[e].astype(F32)).astype(BF16)
        gox[e] = send(go_tx.at[e], go_xrx.at[e], x_dev(e))

    grc[0].wait_recv()
    for e in range(1, nx):
        grx[e, 1].wait_recv()
    gry = {}
    for d in order[1:] + [0]:
        gr_ytx[d] = gr_sum(d, oy).astype(BF16)
        gry[d] = send(gr_ytx.at[d], gr_yrx.at[d], y_dev)

    gsz = {}
    for d in order[1:]:
        gsy[d].wait_recv()
        gs_ztx[d] = (gs[zs(d), y].astype(F32) + gs_yrx[d].astype(F32)).astype(BF16)
        gsz[d] = send(gs_ztx.at[d], gs_zrx.at[d], z_dev(d))

    for e in range(1, nx):
        grx[e, 0].wait_recv()
    grz = {}
    for d in order[1:]:
        gry[d].wait_recv()
        gr_ztx[d] = (gr_sum(d, y) + gr_yrx[d].astype(F32)).astype(BF16)
        grz[d] = send(gr_ztx.at[d], gr_zrx.at[d], z_dev(d))

    goc[0].wait_recv()
    t = go[x, c].astype(F32) + go_crx[0].astype(F32)
    for e in range(1, nx):
        gox[e].wait_recv()
        t = t + go_xrx[e].astype(F32)
    go_out[...] = t
    gsy[0].wait_recv()
    t = gs[z, y].astype(F32) + gs_yrx[0].astype(F32)
    for d in order[1:]:
        gsz[d].wait_recv()
        t = t + gs_zrx[d].astype(F32)
    gs_out[...] = t
    gry[0].wait_recv()
    t = gr_sum(0, y) + gr_yrx[0].astype(F32)
    for d in order[1:]:
        grz[d].wait_recv()
        t = t + gr_zrx[d].astype(F32)
    gr_out[...] = t / (ns * nx * PAIR)
    for cp in started:
        cp.wait_send()


def finish(gs_in, go_in, gr_in, gs_out, go_out, gr_out, loss_out):
    rank = gs_out.shape[1]
    gs_out[...] = gs_in[:, :rank]
    go_out[...] = go_in[...]
    gr_out[...] = gr_in[...]
    loss_out[...] = gs_in[:, rank:].T[0:1, :]


def body(subject_factors, object_factors, relations, labels):
    n_subj, n_obj = lax.axis_size("subj"), lax.axis_size("obj")
    nx, nh = n_subj // PAIR, n_obj // PAIR
    rows_s, rank = subject_factors.shape
    rows_o = object_factors.shape[0]
    rels, rows_r, wid = relations.shape
    ns, no = rows_s * n_obj, rows_o * n_subj
    copies = (nh * (4 + 2 * nx) + 2 * nx) + (3 * nh + 2 * nx + 2 * nx + 2 * nx + 2 * nh)
    v = pltpu.VMEM
    piece = (rels, wid, rows_r)
    scratch = [
        v((nh, PAIR, rows_s, rank), BF16),
        v((nx, PAIR, rows_o, rank), BF16),
        v((nh, PAIR, nx, PAIR) + piece, BF16),
        v((rels, rank, rank), BF16),
        v(labels.shape, jnp.int32),
        v((rels, ns, rank), BF16),
        v((rels, no, rank), BF16),
        v((rels, ns, no), F32),
        v((rels, ns, no), BF16),
        v((rels, ns, rank), BF16),
        v((ns, LANES), F32),
        v((nh, PAIR, nx, PAIR) + piece, BF16),
        v((nx, nh, PAIR) + piece, BF16),
        v((nx, PAIR, nh) + piece, BF16),
        v((nx, PAIR, nh) + piece, BF16),
        v((nh,) + piece, BF16),
        v((nh,) + piece, BF16),
        v((nh,) + piece, BF16),
        v((nh,) + piece, BF16),
        v((nx, PAIR, rows_o, rank), BF16),
        v((nx, rows_o, rank), BF16),
        v((nx, rows_o, rank), BF16),
        v((nx, rows_o, rank), BF16),
        v((nh, PAIR, rows_s, rank + LANES), BF16),
        v((nh, rows_s, rank + LANES), BF16),
        v((nh, rows_s, rank + LANES), BF16),
        v((nh, rows_s, rank + LANES), BF16),
        pltpu.SemaphoreType.DMA((copies,)),
        pltpu.SemaphoreType.DMA((copies,)),
        pltpu.SemaphoreType.DMA((4,)),
    ]
    hbm = pl.BlockSpec(memory_space=pl.ANY)
    vm = pl.BlockSpec(memory_space=pltpu.VMEM)
    sums = pl.pallas_call(
        functools.partial(kernel, nx, nh),
        out_shape=(
            jax.ShapeDtypeStruct((rows_s, rank + LANES), F32),
            jax.ShapeDtypeStruct((rows_o, rank), F32),
            jax.ShapeDtypeStruct(piece, F32),
        ),
        in_specs=[hbm, hbm, hbm, hbm],
        out_specs=(vm, vm, vm),
        scratch_shapes=scratch,
        compiler_params=pltpu.CompilerParams(
            collective_id=0, has_side_effects=True, vmem_limit_bytes=63 * 1024 * 1024
        ),
    )(subject_factors, object_factors, jnp.swapaxes(relations, 1, 2), labels)
    grad_subject, grad_object, grad_relations, loss = pl.pallas_call(
        finish,
        out_shape=(
            jax.ShapeDtypeStruct((rows_s, rank), F32),
            jax.ShapeDtypeStruct((rows_o, rank), F32),
            jax.ShapeDtypeStruct(piece, F32),
            jax.ShapeDtypeStruct((1, rows_s), F32),
        ),
        in_specs=[vm, vm, vm],
        out_specs=(vm, vm, vm, vm),
        compiler_params=pltpu.CompilerParams(vmem_limit_bytes=63 * 1024 * 1024),
    )(*sums)
    return grad_subject, grad_object, jnp.swapaxes(grad_relations, 1, 2), loss.reshape(rows_s)


def solution(mesh):
    placed = (
        P(("subj", "obj"), None),
        P(("obj", "subj"), None),
        P(None, "subj", "obj"),
        P(None, "subj", "obj"),
    )
    return jax.shard_map(
        body,
        mesh=mesh,
        in_specs=placed,
        out_specs=(
            P(("subj", "obj"), None),
            P(("obj", "subj"), None),
            P(None, "subj", "obj"),
            P(("subj", "obj")),
        ),
        check_vma=False,
    )
```

```python
import functools

import jax
import jax.numpy as jnp
from jax import lax
from jax.experimental import pallas as pl
from jax.experimental.pallas import tpu as pltpu
from jax.sharding import PartitionSpec as P

F32 = jnp.float32
BF16 = jnp.bfloat16
PAIR = 2
LANES = 128
TILE = 16
CHUNK = 64


def mm(a, b, ca, cb):
    return lax.dot_general(a, b, (((ca,), (cb,)), ((), ())), preferred_element_type=F32)


def kernel(
    nx, nh,
    s_hbm, o_hbm, r_hbm, lab_hbm,
    gs_out, go_out, gr_out, loss_out,
    s_all, o_all, r_all, r_full, labels, left, right, score, resid,
    loss, gr, gr_crx, gr_tx, gr_xrx, gr_ytx, gr_yrx, gr_ztx, gr_zrx,
    go, go_crx, go_tx, go_xrx, gs, gs_yrx, gs_ztx, gs_zrx,
    ls, ls_yrx, ls_ztx, ls_zrx,
    send_sem, recv_sem, local_sem,
):
    subj = lax.axis_index("subj")
    obj = lax.axis_index("obj")
    x, c = subj // PAIR, subj % PAIR
    z, y = obj // PAIR, obj % PAIR
    oc, oy = 1 - c, 1 - y
    rels, rank = r_full.shape[0], r_full.shape[1]
    wid, rows_r = r_hbm.shape[1], r_hbm.shape[2]
    rows_s = s_all.shape[2]
    ns = nh * PAIR * rows_s
    no = nx * PAIR * o_all.shape[2]
    core_dev = (x * PAIR + oc, obj)
    y_dev = (subj, z * PAIR + oy)

    def xs(e):
        return lax.rem(x + e, nx)

    def zs(d):
        return lax.rem(z + d, nh)

    def x_from(e):
        return lax.rem(x - e + nx, nx)

    def z_from(d):
        return lax.rem(z - d + nh, nh)

    def x_dev(e):
        return (xs(e) * PAIR + c, obj)

    def z_dev(d):
        return (subj, zs(d) * PAIR + y)

    started = []

    def send(src, dst, dev):
        i = len(started)
        cp = pltpu.make_async_remote_copy(
            src_ref=src, dst_ref=dst, send_sem=send_sem.at[i], recv_sem=recv_sem.at[i],
            device_id=dev, device_id_type=pl.DeviceIdType.MESH,
        )
        cp.start()
        started.append(cp)
        return cp

    barrier = pltpu.get_barrier_semaphore()
    partners = [core_dev, y_dev] + [x_dev(e) for e in range(1, nx)] + [z_dev(d) for d in range(1, nh)]
    for dev in partners:
        pl.semaphore_signal(barrier, inc=1, device_id=dev, device_id_type=pl.DeviceIdType.MESH)

    r_cp = pltpu.make_async_copy(r_hbm, r_all.at[z, y, x, c], local_sem.at[3])
    r_cp.start()
    s_cp = pltpu.make_async_copy(s_hbm, s_all.at[z, y], local_sem.at[1])
    s_cp.start()
    o_cp = pltpu.make_async_copy(o_hbm, o_all.at[x, c], local_sem.at[2])
    o_cp.start()
    lab_cp = pltpu.make_async_copy(lab_hbm, labels, local_sem.at[0])
    lab_cp.start()
    loss[...] = jnp.zeros_like(loss)
    ls[...] = jnp.zeros_like(ls)
    pl.semaphore_wait(barrier, len(partners))

    order = [d for d in range(nh)]
    rz, sz = {}, {}
    for d in range(1, nh):
        rz[d] = send(r_hbm, r_all.at[z, y, x, c], z_dev(d))
    ry, sy = {}, {}
    ry[0] = send(r_hbm, r_all.at[z, y, x, c], y_dev)
    ox = {e: send(o_hbm, o_all.at[x, c], x_dev(e)) for e in range(1, nx)}
    ocr = {0: send(o_hbm, o_all.at[x, c], core_dev)}
    for d in range(1, nh):
        sz[d] = send(s_hbm, s_all.at[z, y], z_dev(d))
    sy[0] = send(s_hbm, s_all.at[z, y], y_dev)
    r_cp.wait()
    rx, rc = {}, {}

    def spread(d):
        ry[d].wait_recv()
        blk = r_all.at[z_from(d), :, x, c]
        for e in range(1, nx):
            rx[d, e] = send(blk, blk, x_dev(e))
        rc[d, 0] = send(blk, blk, core_dev)

    for d in order:
        if d:
            rz[d].wait_recv()
            blk = r_all.at[z_from(d), y, x, c]
            ry[d] = send(blk, blk, y_dev)
        if d != 1:
            spread(d - 1 if d else 0)
    if nh > 1:
        spread(nh - 1)
    for e in range(1, nx):
        ox[e].wait_recv()
        blk = o_all.at[x_from(e), c]
        ocr[e] = send(blk, blk, core_dev)
    for d in order:
        for e in range(1, nx):
            rx[d, e].wait_recv()
            blk = r_all.at[z_from(d), :, x_from(e), c]
            rc[d, e] = send(blk, blk, core_dev)
        if d:
            sz[d].wait_recv()
            blk = s_all.at[z_from(d), y]
            sy[d] = send(blk, blk, y_dev)
    for key in rc:
        rc[key].wait_recv()
    for s in range(nx * PAIR):
        for k in range(rels):
            r_full[k, :, s * rows_r:(s + 1) * rows_r] = (
                r_all[:, :, s // PAIR, s % PAIR, k].reshape(rank, rows_r))
    o_cp.wait()
    for e in range(nx):
        ocr[e].wait_recv()
    for k in range(rels):
        right[k] = mm(o_all[...].reshape(no, rank), r_full[k], 1, 0).astype(BF16)
    s_cp.wait()
    for d in order:
        sy[d].wait_recv()
    lab_cp.wait()
    turns = list(range(1, nx)) + [0]
    grc, grx = {}, {}

    def gr_along_x(k):
        for e in range(1, nx):
            grc[k, e].wait_recv()
            for first in (1, 0):
                q = oy if first else y
                gr_tx[e, q, k] = (
                    gr[k, :, q, xs(e), c].astype(F32) + gr_crx[k, e, :, q].astype(F32)).astype(BF16)
                grx[k, e, first] = send(gr_tx.at[e, q, k], gr_xrx.at[e, q, k], x_dev(e))

    for k in range(rels):
        left[k] = mm(s_all[...].reshape(ns, rank), r_full[k], 1, 1).astype(BF16)
        score[...] = mm(left[k], o_all[...].reshape(no, rank), 1, 1)

        def rows_body(i, carry, k=k):
            r = pl.ds(pl.multiple_of(i * CHUNK, CHUNK), CHUNK)
            sc = score[r, :]
            codes = labels[k, r, :]
            target = jnp.where(codes == 2, 1.0, 0.0).astype(F32)
            held = codes > 0
            e = jnp.exp(-jnp.abs(sc))
            inv = 1.0 / (1.0 + e)
            sig = jnp.where(sc >= 0, inv, e * inv)
            soft = jnp.maximum(sc, 0.0) + jnp.log1p(e)
            cell = jnp.where(held, soft - target * sc, 0.0)
            part = loss[r, :]
            for g in range(no // LANES):
                part = part + cell[:, g * LANES:(g + 1) * LANES]
            loss[r, :] = part
            resid[k, r, :] = jnp.where(held, sig - target, 0.0).astype(BF16)
            return carry
        lax.fori_loop(0, ns // CHUNK, rows_body, 0)
        carried = mm(resid[k], o_all[...].reshape(no, rank), 1, 0).astype(BF16)
        term = mm(carried, s_all[...].reshape(ns, rank), 0, 0).astype(BF16)
        for s in range(nx * PAIR):
            gr[k, :, :, s // PAIR, s % PAIR] = (
                term[:, s * rows_r:(s + 1) * rows_r].reshape(nh, PAIR, wid, rows_r))
        for e in turns:
            grc[k, e] = send(gr.at[k, :, :, xs(e), oc], gr_crx.at[k, e], core_dev)
        if k:
            gr_along_x(k - 1)

    acc = None
    for k in range(rels):
        t = mm(resid[k], right[k], 1, 0)
        acc = t if acc is None else acc + t
    objects = no * nh * PAIR
    gs[...] = acc.astype(BF16).reshape(nh, PAIR, rows_s, rank)
    gsy = {}
    for d in order[1:] + [0]:
        gsy[d] = send(gs.at[zs(d), oy], gs_yrx.at[d], y_dev)
    gr_along_x(rels - 1)
    row_loss = jnp.sum(loss[...].T, axis=0, keepdims=True) / (rels * objects)
    for o in range(nh * PAIR):
        ls[o % PAIR, o // PAIR, :, :rows_s] = jnp.broadcast_to(
            row_loss[:, o * rows_s:(o + 1) * rows_s], (TILE, rows_s)).astype(BF16)
    lsy = send(ls.at[oy], ls_yrx, y_dev)

    acc = None
    for k in range(rels):
        t = mm(resid[k], left[k], 0, 0)
        acc = t if acc is None else acc + t
    go[...] = acc.astype(BF16).reshape(go.shape)
    goc = {}
    for e in turns:
        goc[e] = send(go.at[xs(e), oc], go_crx.at[e], core_dev)

    def gr_sum(d, q):
        t = gr[:, zs(d), q, x, c].astype(F32) + gr_crx[:, 0, zs(d), q].astype(F32)
        for e in range(1, nx):
            t = t + gr_xrx[e, q, :, zs(d)].astype(F32)
        return t

    gox = {}
    for e in range(1, nx):
        goc[e].wait_recv()
        go_tx[e] = (go[xs(e), c].astype(F32) + go_crx[e].astype(F32)).astype(BF16)
        gox[e] = send(go_tx.at[e], go_xrx.at[e], x_dev(e))

    for k in range(rels):
        grc[k, 0].wait_recv()
        for e in range(1, nx):
            grx[k, e, 1].wait_recv()
    gry = {}
    for d in order[1:] + [0]:
        gr_ytx[d] = gr_sum(d, oy).astype(BF16)
        gry[d] = send(gr_ytx.at[d], gr_yrx.at[d], y_dev)

    gsz = {}
    for d in order[1:]:
        gsy[d].wait_recv()
        gs_ztx[d] = (gs[zs(d), y].astype(F32) + gs_yrx[d].astype(F32)).astype(BF16)
        gsz[d] = send(gs_ztx.at[d], gs_zrx.at[d], z_dev(d))

    lsy.wait_recv()
    lsz = {}
    for d in order[1:]:
        ls_ztx[d] = (ls[y, zs(d)].astype(F32) + ls_yrx[zs(d)].astype(F32)).astype(BF16)
        lsz[d] = send(ls_ztx.at[d], ls_zrx.at[d], z_dev(d))

    for k in range(rels):
        for e in range(1, nx):
            grx[k, e, 0].wait_recv()
    grz = {}
    for d in order[1:]:
        gry[d].wait_recv()
        gr_ztx[d] = (gr_sum(d, y) + gr_yrx[d].astype(F32)).astype(BF16)
        grz[d] = send(gr_ztx.at[d], gr_zrx.at[d], z_dev(d))

    goc[0].wait_recv()
    t = go[x, c].astype(F32) + go_crx[0].astype(F32)
    for e in range(1, nx):
        gox[e].wait_recv()
        t = t + go_xrx[e].astype(F32)
    go_out[...] = t
    gsy[0].wait_recv()
    t = gs[z, y].astype(F32) + gs_yrx[0].astype(F32)
    for d in order[1:]:
        gsz[d].wait_recv()
        t = t + gs_zrx[d].astype(F32)
    gs_out[...] = t
    t = ls[y, z].astype(F32) + ls_yrx[z].astype(F32)
    for d in order[1:]:
        lsz[d].wait_recv()
        t = t + ls_zrx[d].astype(F32)
    loss_out[...] = t[0:1, :rows_s]
    gry[0].wait_recv()
    t = gr_sum(0, y) + gr_yrx[0].astype(F32)
    for d in order[1:]:
        grz[d].wait_recv()
        t = t + gr_zrx[d].astype(F32)
    gr_out[...] = t / (ns * nx * PAIR)
    for cp in started:
        cp.wait_send()


def finish(*refs):
    count = len(refs) // 2
    sem = refs[-1]
    moves = [pltpu.make_async_copy(refs[i], refs[count + i], sem.at[i]) for i in range(count)]
    for m in moves:
        m.start()
    for m in moves:
        m.wait()


def body(subject_factors, object_factors, relations, labels):
    n_subj, n_obj = lax.axis_size("subj"), lax.axis_size("obj")
    nx, nh = n_subj // PAIR, n_obj // PAIR
    rows_s, rank = subject_factors.shape
    rows_o = object_factors.shape[0]
    rels, rows_r, wid = relations.shape
    ns, no = rows_s * n_obj, rows_o * n_subj
    copies = nh * (4 + 2 * nx) + 2 * nx + 5 * nh + 2 * nx + rels * 3 * nx + nh
    lw = -(-rows_s // LANES) * LANES
    v = pltpu.VMEM
    piece = (rels, wid, rows_r)
    scratch = [
        v((nh, PAIR, rows_s, rank), BF16),
        v((nx, PAIR, rows_o, rank), BF16),
        v((nh, PAIR, nx, PAIR) + piece, BF16),
        v((rels, rank, rank), BF16),
        v(labels.shape, jnp.int32),
        v((rels, ns, rank), BF16),
        v((rels, no, rank), BF16),
        v((ns, no), F32),
        v((rels, ns, no), BF16),
        v((ns, LANES), F32),
        v((rels, nh, PAIR, nx, PAIR, wid, rows_r), BF16),
        v((rels, nx, nh, PAIR, wid, rows_r), BF16),
        v((nx, PAIR, rels, nh, wid, rows_r), BF16),
        v((nx, PAIR, rels, nh, wid, rows_r), BF16),
        v((nh,) + piece, BF16),
        v((nh,) + piece, BF16),
        v((nh,) + piece, BF16),
        v((nh,) + piece, BF16),
        v((nx, PAIR, rows_o, rank), BF16),
        v((nx, rows_o, rank), BF16),
        v((nx, rows_o, rank), BF16),
        v((nx, rows_o, rank), BF16),
        v((nh, PAIR, rows_s, rank), BF16),
        v((nh, rows_s, rank), BF16),
        v((nh, rows_s, rank), BF16),
        v((nh, rows_s, rank), BF16),
        v((PAIR, nh, TILE, lw), BF16),
        v((nh, TILE, lw), BF16),
        v((nh, TILE, lw), BF16),
        v((nh, TILE, lw), BF16),
        pltpu.SemaphoreType.DMA((copies,)),
        pltpu.SemaphoreType.DMA((copies,)),
        pltpu.SemaphoreType.DMA((4,)),
    ]
    hbm = pl.BlockSpec(memory_space=pl.ANY)
    vm = pl.BlockSpec(memory_space=pltpu.VMEM)
    results = (
        jax.ShapeDtypeStruct((rows_s, rank), F32),
        jax.ShapeDtypeStruct((rows_o, rank), F32),
        jax.ShapeDtypeStruct(piece, F32),
        jax.ShapeDtypeStruct((1, rows_s), F32),
    )
    sums = pl.pallas_call(
        functools.partial(kernel, nx, nh),
        out_shape=results,
        in_specs=[hbm, hbm, hbm, hbm],
        out_specs=(vm, vm, vm, vm),
        scratch_shapes=scratch,
        compiler_params=pltpu.CompilerParams(
            collective_id=0, has_side_effects=True, vmem_limit_bytes=63 * 1024 * 1024
        ),
    )(subject_factors, object_factors, jnp.swapaxes(relations, 1, 2), labels)
    grad_subject, grad_object, grad_relations, loss = pl.pallas_call(
        finish,
        out_shape=results,
        in_specs=[hbm] * 4,
        out_specs=(hbm,) * 4,
        scratch_shapes=[pltpu.SemaphoreType.DMA((4,))],
        compiler_params=pltpu.CompilerParams(vmem_limit_bytes=63 * 1024 * 1024),
    )(*sums)
    return grad_subject, grad_object, jnp.swapaxes(grad_relations, 1, 2), loss.reshape(rows_s)


def solution(mesh):
    placed = (
        P(("subj", "obj"), None),
        P(("obj", "subj"), None),
        P(None, "subj", "obj"),
        P(None, "subj", "obj"),
    )
    return jax.shard_map(
        body,
        mesh=mesh,
        in_specs=placed,
        out_specs=(
            P(("subj", "obj"), None),
            P(("obj", "subj"), None),
            P(None, "subj", "obj"),
            P(("subj", "obj")),
        ),
        check_vma=False,
    )
```

```python
import functools

import jax
import jax.numpy as jnp
from jax import lax
from jax.experimental import pallas as pl
from jax.experimental.pallas import tpu as pltpu
from jax.sharding import PartitionSpec as P

F32 = jnp.float32
BF16 = jnp.bfloat16
PAIR = 2
LANES = 128
TILE = 16
CHUNK = 64


def mm(a, b, ca, cb):
    return lax.dot_general(a, b, (((ca,), (cb,)), ((), ())), preferred_element_type=F32)


def kernel(
    nx, nh,
    s_hbm, o_hbm, r_hbm, lab_hbm,
    gs_out, go_out, gr_out, loss_out,
    s_all, o_all, r_all, r_full, labels, left, right, score, resid,
    loss, gr, gr_crx, gr_tx, gr_xrx, gr_ytx, gr_yrx, gr_ztx, gr_zrx,
    go, go_crx, go_tx, go_xrx, gs, gs_yrx, gs_ztx, gs_zrx,
    ls, ls_yrx, ls_ztx, ls_zrx,
    send_sem, recv_sem, local_sem,
):
    subj = lax.axis_index("subj")
    obj = lax.axis_index("obj")
    x, c = subj // PAIR, subj % PAIR
    z, y = obj // PAIR, obj % PAIR
    oc, oy = 1 - c, 1 - y
    rels, rank = r_full.shape[0], r_full.shape[1]
    wid, rows_r = r_hbm.shape[1], r_hbm.shape[2]
    rows_s = s_all.shape[2]
    ns = nh * PAIR * rows_s
    no = nx * PAIR * o_all.shape[2]
    core_dev = (x * PAIR + oc, obj)
    y_dev = (subj, z * PAIR + oy)

    def xs(e):
        return lax.rem(x + e, nx)

    def zs(d):
        return lax.rem(z + d, nh)

    def x_from(e):
        return lax.rem(x - e + nx, nx)

    def z_from(d):
        return lax.rem(z - d + nh, nh)

    def x_dev(e):
        return (xs(e) * PAIR + c, obj)

    def z_dev(d):
        return (subj, zs(d) * PAIR + y)

    started = []

    def send(src, dst, dev):
        i = len(started)
        cp = pltpu.make_async_remote_copy(
            src_ref=src, dst_ref=dst, send_sem=send_sem.at[i], recv_sem=recv_sem.at[i],
            device_id=dev, device_id_type=pl.DeviceIdType.MESH,
        )
        cp.start()
        started.append(cp)
        return cp

    barrier = pltpu.get_barrier_semaphore()
    partners = [core_dev, y_dev] + [x_dev(e) for e in range(1, nx)] + [z_dev(d) for d in range(1, nh)]
    for dev in partners:
        pl.semaphore_signal(barrier, inc=1, device_id=dev, device_id_type=pl.DeviceIdType.MESH)

    r_cp = pltpu.make_async_copy(r_hbm, r_all.at[z, y, x, c], local_sem.at[3])
    r_cp.start()
    s_cp = pltpu.make_async_copy(s_hbm, s_all.at[z, y], local_sem.at[1])
    s_cp.start()
    o_cp = pltpu.make_async_copy(o_hbm, o_all.at[x, c], local_sem.at[2])
    o_cp.start()
    lab_cp = pltpu.make_async_copy(lab_hbm, labels, local_sem.at[0])
    lab_cp.start()
    loss[...] = jnp.zeros_like(loss)
    ls[...] = jnp.zeros_like(ls)
    pl.semaphore_wait(barrier, len(partners))

    order = [d for d in range(nh)]
    r_mine, s_mine, o_mine = r_all.at[z, y, x, c], s_all.at[z, y], o_all.at[x, c]
    r_cp.wait()
    rz, sz = {}, {}
    for d in range(1, nh):
        rz[d] = send(r_mine, r_mine, z_dev(d))
    ry, sy = {}, {}
    ry[0] = send(r_mine, r_mine, y_dev)
    o_cp.wait()
    ox = {e: send(o_mine, o_mine, x_dev(e)) for e in range(1, nx)}
    ocr = {0: send(o_mine, o_mine, core_dev)}
    s_cp.wait()
    for d in range(1, nh):
        sz[d] = send(s_mine, s_mine, z_dev(d))
    sy[0] = send(s_mine, s_mine, y_dev)
    rx, rc = {}, {}

    def spread(d):
        ry[d].wait_recv()
        blk = r_all.at[z_from(d), :, x, c]
        for e in range(1, nx):
            rx[d, e] = send(blk, blk, x_dev(e))
        rc[d, 0] = send(blk, blk, core_dev)

    for d in order:
        if d:
            rz[d].wait_recv()
            blk = r_all.at[z_from(d), y, x, c]
            ry[d] = send(blk, blk, y_dev)
        if d != 1:
            spread(d - 1 if d else 0)
    if nh > 1:
        spread(nh - 1)
    for e in range(1, nx):
        ox[e].wait_recv()
        blk = o_all.at[x_from(e), c]
        ocr[e] = send(blk, blk, core_dev)
    for d in order:
        for e in range(1, nx):
            rx[d, e].wait_recv()
            blk = r_all.at[z_from(d), :, x_from(e), c]
            rc[d, e] = send(blk, blk, core_dev)
        if d:
            sz[d].wait_recv()
            blk = s_all.at[z_from(d), y]
            sy[d] = send(blk, blk, y_dev)
    for key in rc:
        rc[key].wait_recv()
    for s in range(nx * PAIR):
        for k in range(rels):
            r_full[k, :, s * rows_r:(s + 1) * rows_r] = (
                r_all[:, :, s // PAIR, s % PAIR, k].reshape(rank, rows_r))
    for e in range(nx):
        ocr[e].wait_recv()
    for k in range(rels):
        right[k] = mm(o_all[...].reshape(no, rank), r_full[k], 1, 0).astype(BF16)
    for d in order:
        sy[d].wait_recv()
    lab_cp.wait()
    turns = list(range(1, nx)) + [0]
    grc, grx = {}, {}

    def gr_along_x(k):
        for e in range(1, nx):
            grc[k, e].wait_recv()
            for first in (1, 0):
                q = oy if first else y
                gr_tx[e, q, k] = (
                    gr[k, :, q, xs(e), c].astype(F32) + gr_crx[k, e, :, q].astype(F32)).astype(BF16)
                grx[k, e, first] = send(gr_tx.at[e, q, k], gr_xrx.at[e, q, k], x_dev(e))

    for k in range(rels):
        left[k] = mm(s_all[...].reshape(ns, rank), r_full[k], 1, 1).astype(BF16)
        score[...] = mm(left[k], o_all[...].reshape(no, rank), 1, 1)

        def rows_body(i, carry, k=k):
            r = pl.ds(pl.multiple_of(i * CHUNK, CHUNK), CHUNK)
            sc = score[r, :]
            codes = labels[k, r, :]
            target = jnp.where(codes == 2, 1.0, 0.0).astype(F32)
            held = codes > 0
            e = jnp.exp(-jnp.abs(sc))
            tail = jnp.where(e < 2.0 ** -8, e - 0.5 * e * e, jnp.log(1.0 + e))
            sig = jnp.exp(jnp.minimum(sc, 0.0) - tail)
            soft = jnp.maximum(sc, 0.0) + tail
            cell = jnp.where(held, soft - target * sc, 0.0)
            part = loss[r, :]
            for g in range(no // LANES):
                part = part + cell[:, g * LANES:(g + 1) * LANES]
            loss[r, :] = part
            resid[k, r, :] = jnp.where(held, sig - target, 0.0).astype(BF16)
            return carry
        lax.fori_loop(0, ns // CHUNK, rows_body, 0)
        carried = mm(resid[k], o_all[...].reshape(no, rank), 1, 0).astype(BF16)
        term = mm(carried, s_all[...].reshape(ns, rank), 0, 0).astype(BF16)
        for s in range(nx * PAIR):
            gr[k, :, :, s // PAIR, s % PAIR] = (
                term[:, s * rows_r:(s + 1) * rows_r].reshape(nh, PAIR, wid, rows_r))
        for e in turns:
            grc[k, e] = send(gr.at[k, :, :, xs(e), oc], gr_crx.at[k, e], core_dev)
        if k:
            gr_along_x(k - 1)

    acc = None
    for k in range(rels):
        t = mm(resid[k], right[k], 1, 0)
        acc = t if acc is None else acc + t
    objects = no * nh * PAIR
    gs[...] = acc.astype(BF16).reshape(nh, PAIR, rows_s, rank)
    gsy = {}
    for d in order[1:] + [0]:
        gsy[d] = send(gs.at[zs(d), oy], gs_yrx.at[d], y_dev)
    gr_along_x(rels - 1)
    row_loss = jnp.sum(loss[...].T, axis=0, keepdims=True) / (rels * objects)
    for o in range(nh * PAIR):
        ls[o % PAIR, o // PAIR, :, :rows_s] = jnp.broadcast_to(
            row_loss[:, o * rows_s:(o + 1) * rows_s], (TILE, rows_s)).astype(BF16)
    lsy = send(ls.at[oy], ls_yrx, y_dev)

    acc = None
    for k in range(rels):
        t = mm(resid[k], left[k], 0, 0)
        acc = t if acc is None else acc + t
    go[...] = acc.astype(BF16).reshape(go.shape)
    goc = {}
    for e in turns:
        goc[e] = send(go.at[xs(e), oc], go_crx.at[e], core_dev)

    def gr_sum(d, q):
        t = gr[:, zs(d), q, x, c].astype(F32) + gr_crx[:, 0, zs(d), q].astype(F32)
        for e in range(1, nx):
            t = t + gr_xrx[e, q, :, zs(d)].astype(F32)
        return t

    gox = {}
    for e in range(1, nx):
        goc[e].wait_recv()
        go_tx[e] = (go[xs(e), c].astype(F32) + go_crx[e].astype(F32)).astype(BF16)
        gox[e] = send(go_tx.at[e], go_xrx.at[e], x_dev(e))

    for k in range(rels):
        grc[k, 0].wait_recv()
        for e in range(1, nx):
            grx[k, e, 1].wait_recv()
    gry = {}
    for d in order[1:] + [0]:
        gr_ytx[d] = gr_sum(d, oy).astype(BF16)
        gry[d] = send(gr_ytx.at[d], gr_yrx.at[d], y_dev)

    gsz = {}
    for d in order[1:]:
        gsy[d].wait_recv()
        gs_ztx[d] = (gs[zs(d), y].astype(F32) + gs_yrx[d].astype(F32)).astype(BF16)
        gsz[d] = send(gs_ztx.at[d], gs_zrx.at[d], z_dev(d))

    lsy.wait_recv()
    lsz = {}
    for d in order[1:]:
        ls_ztx[d] = (ls[y, zs(d)].astype(F32) + ls_yrx[zs(d)].astype(F32)).astype(BF16)
        lsz[d] = send(ls_ztx.at[d], ls_zrx.at[d], z_dev(d))

    for k in range(rels):
        for e in range(1, nx):
            grx[k, e, 0].wait_recv()
    grz = {}
    for d in order[1:]:
        gry[d].wait_recv()
        gr_ztx[d] = (gr_sum(d, y) + gr_yrx[d].astype(F32)).astype(BF16)
        grz[d] = send(gr_ztx.at[d], gr_zrx.at[d], z_dev(d))

    goc[0].wait_recv()
    t = go[x, c].astype(F32) + go_crx[0].astype(F32)
    for e in range(1, nx):
        gox[e].wait_recv()
        t = t + go_xrx[e].astype(F32)
    go_out[...] = t
    gsy[0].wait_recv()
    t = gs[z, y].astype(F32) + gs_yrx[0].astype(F32)
    for d in order[1:]:
        gsz[d].wait_recv()
        t = t + gs_zrx[d].astype(F32)
    gs_out[...] = t
    t = ls[y, z].astype(F32) + ls_yrx[z].astype(F32)
    for d in order[1:]:
        lsz[d].wait_recv()
        t = t + ls_zrx[d].astype(F32)
    loss_out[...] = t[0:1, :rows_s]
    gry[0].wait_recv()
    t = gr_sum(0, y) + gr_yrx[0].astype(F32)
    for d in order[1:]:
        grz[d].wait_recv()
        t = t + gr_zrx[d].astype(F32)
    gr_out[...] = t / (ns * nx * PAIR)
    for cp in started:
        cp.wait_send()


def finish(gs_in, go_in, gr_in, loss_in, gs_out, go_out, gr_out, loss_out):
    gs_out[...] = gs_in[...]
    go_out[...] = go_in[...]
    gr_out[...] = gr_in[...]
    loss_out[...] = loss_in[...]


def body(subject_factors, object_factors, relations, labels):
    n_subj, n_obj = lax.axis_size("subj"), lax.axis_size("obj")
    nx, nh = n_subj // PAIR, n_obj // PAIR
    rows_s, rank = subject_factors.shape
    rows_o = object_factors.shape[0]
    rels, rows_r, wid = relations.shape
    ns, no = rows_s * n_obj, rows_o * n_subj
    copies = nh * (4 + 2 * nx) + 2 * nx + 5 * nh + 2 * nx + rels * 3 * nx + nh
    lw = -(-rows_s // LANES) * LANES
    v = pltpu.VMEM
    piece = (rels, wid, rows_r)
    scratch = [
        v((nh, PAIR, rows_s, rank), BF16),
        v((nx, PAIR, rows_o, rank), BF16),
        v((nh, PAIR, nx, PAIR) + piece, BF16),
        v((rels, rank, rank), BF16),
        v(labels.shape, jnp.int32),
        v((rels, ns, rank), BF16),
        v((rels, no, rank), BF16),
        v((ns, no), F32),
        v((rels, ns, no), BF16),
        v((ns, LANES), F32),
        v((rels, nh, PAIR, nx, PAIR, wid, rows_r), BF16),
        v((rels, nx, nh, PAIR, wid, rows_r), BF16),
        v((nx, PAIR, rels, nh, wid, rows_r), BF16),
        v((nx, PAIR, rels, nh, wid, rows_r), BF16),
        v((nh,) + piece, BF16),
        v((nh,) + piece, BF16),
        v((nh,) + piece, BF16),
        v((nh,) + piece, BF16),
        v((nx, PAIR, rows_o, rank), BF16),
        v((nx, rows_o, rank), BF16),
        v((nx, rows_o, rank), BF16),
        v((nx, rows_o, rank), BF16),
        v((nh, PAIR, rows_s, rank), BF16),
        v((nh, rows_s, rank), BF16),
        v((nh, rows_s, rank), BF16),
        v((nh, rows_s, rank), BF16),
        v((PAIR, nh, TILE, lw), BF16),
        v((nh, TILE, lw), BF16),
        v((nh, TILE, lw), BF16),
        v((nh, TILE, lw), BF16),
        pltpu.SemaphoreType.DMA((copies,)),
        pltpu.SemaphoreType.DMA((copies,)),
        pltpu.SemaphoreType.DMA((4,)),
    ]
    hbm = pl.BlockSpec(memory_space=pl.ANY)
    vm = pl.BlockSpec(memory_space=pltpu.VMEM)
    results = (
        jax.ShapeDtypeStruct((rows_s, rank), F32),
        jax.ShapeDtypeStruct((rows_o, rank), F32),
        jax.ShapeDtypeStruct(piece, F32),
        jax.ShapeDtypeStruct((1, rows_s), F32),
    )
    sums = pl.pallas_call(
        functools.partial(kernel, nx, nh),
        out_shape=results,
        in_specs=[hbm, hbm, hbm, hbm],
        out_specs=(vm, vm, vm, vm),
        scratch_shapes=scratch,
        compiler_params=pltpu.CompilerParams(
            collective_id=0, has_side_effects=True, vmem_limit_bytes=63 * 1024 * 1024
        ),
    )(subject_factors, object_factors, jnp.swapaxes(relations, 1, 2), labels)
    grad_subject, grad_object, grad_relations, loss = pl.pallas_call(
        finish,
        out_shape=results,
        in_specs=[vm] * 4,
        out_specs=(vm,) * 4,
        compiler_params=pltpu.CompilerParams(vmem_limit_bytes=63 * 1024 * 1024),
    )(*sums)
    return grad_subject, grad_object, jnp.swapaxes(grad_relations, 1, 2), loss.reshape(rows_s)


def solution(mesh):
    placed = (
        P(("subj", "obj"), None),
        P(("obj", "subj"), None),
        P(None, "subj", "obj"),
        P(None, "subj", "obj"),
    )
    return jax.shard_map(
        body,
        mesh=mesh,
        in_specs=placed,
        out_specs=(
            P(("subj", "obj"), None),
            P(("obj", "subj"), None),
            P(None, "subj", "obj"),
            P(("subj", "obj")),
        ),
        check_vma=False,
    )
```
